32 devices in a mesh: groups: 2 (over y), dp: 4 (over z), mp: 4 (over x, core).
Axes of the slice: x: 2, y: 2, z: 4, core: 2. Of those that a mesh axis runs over, the one named last changes fastest.
Arguments:
- acts: bfloat16 [4096, 2304], P(('groups', 'dp')), parts along dimension 0, may hold values from -6 to 6
- out_grads: bfloat16 [4096, 18432], P(('groups', 'dp'), 'mp'), parts along dimension 0, may hold values from -6 to 6
- lengths: int32 [8, 4], P(('groups', 'dp')), parts along dimension 0, may hold values from 1 to 256, 512 in all within a row
Outputs:
- clipped_grad: float32 [4608, 18432], P(('groups', 'dp'), 'mp'), parts along dimension 0
- seq_norms: float32 [8, 4], P(('groups', 'dp')), parts along dimension 0
The draws below stay inside these ranges and needn't reach their ends.
There are 2 independent parts, one for each index of `groups`. The reference program is written for one: setup_inputs(seed, part) draws one part's arguments, and reference() takes and returns one part's arrays. A program takes and returns all parts, laid end to end along the dimension named above; each array names one. Nothing has to cross between parts.
Inputs may be any that keep to these rules, and one draw needn't show every extreme that they name: `lengths`: each row sums to 512; every row has an entry equal to 256.
All inputs are finite; a program needn't handle non-finite values.
Results may differ from the reference program's by a relative error of at most 0.0028.
Values may be sent and summed in bfloat16 or wider, within the bound.
No kernel may reach another device: no remote copies, remote signals or barrier semaphores. Data moves between devices by JAX's collectives and lax.ppermute only.
A program may use at most 192 MiB of HBM per device.

```python
import math
import jax
import jax.numpy as jnp
import numpy as np
from jax import lax

D = 2304
FFW = 18432
TOK_DEV = 512
SEG_DEV = 4
MOST = 256
BLOCKS = 4
TOKENS = 2048
SEQS = 16


def block_scale(key, extent, shards, least, top_value):
    gain, own = 1.0, jax.random.fold_in(key, 6)
    for axis_at, parts in shards:
        steps = jnp.exp(jax.random.uniform(jax.random.fold_in(own, axis_at), (parts,), jnp.float32, least / len(shards), top_value / len(shards)))
        gain = gain * jnp.repeat(steps, extent[axis_at] // parts).reshape([-1 if axis == axis_at else 1 for axis in range(len(extent))])
    return gain


def split_up(amount, total, most, skew):
    portions = [(1 << 20) // math.isqrt(grade ** skew) + 1 for grade in range(2, amount + 1)]
    surplus, counts = total - most - (amount - 1), [1] * (amount - 1)
    while surplus > 0:
        free = [i for i in range(amount - 1) if counts[i] < most]
        mass, budget = sum([portions[i] for i in free]), surplus
        for i in free:
            addition = min(most - counts[i], max(1, budget * portions[i] // mass), surplus)
            counts[i] = counts[i] + addition
            surplus = surplus - addition
    return np.array([most] + counts)


def ragged_sizes(own_key, amount, total, limit, lean):
    if amount == 2:
        one = jax.random.randint(own_key, (), max(1, total - limit), min(limit, total - 1) + 1)
        return jnp.stack([one, total - one])
    sizes = jnp.asarray(split_up(amount, total, limit, lean), jnp.int32)
    twos = (amount - 1) // 2
    source_of, receiver = sizes[1:1 + 2 * twos:2], sizes[2:2 + 2 * twos:2]
    margin = jnp.minimum(source_of - 1, limit - receiver)
    passed = jax.random.randint(jax.random.fold_in(own_key, 1), (twos,), 0, 1 << 20) % (margin + 1)
    sizes = sizes.at[1:1 + 2 * twos:2].set(source_of - passed).at[2:2 + 2 * twos:2].set(receiver + passed)
    return sizes[jax.random.permutation(jax.random.fold_in(own_key, 2), amount)]


def gaussian(key, extent, deviation, reach, cuts=(), kind=jnp.bfloat16):
    values = deviation * jax.random.normal(key, extent, jnp.float32)
    if cuts:
        values = values * block_scale(key, extent, cuts, -0.22, 0.18)
    return jnp.clip(values, -reach, reach).astype(kind)


def setup_inputs(seed: int = 0, part: int = 0) -> dict:
    key_of = jax.random.split(jax.random.key(seed), 4)
    part_splits = jax.random.split(jax.random.fold_in(key_of[3], part), 4)
    acts = gaussian(part_splits[0], (TOKENS, D), 1.0, 6.0, ((0, 4),))
    out_grads = gaussian(part_splits[1], (TOKENS, FFW), 1.0, 6.0, ((0, 4), (1, 4)))
    lengths = jax.vmap(lambda own: ragged_sizes(own, SEG_DEV, TOK_DEV, MOST, 2))(jax.random.split(part_splits[2], BLOCKS)).reshape((BLOCKS, SEG_DEV)).astype(jnp.int32)
    return dict(acts=acts, out_grads=out_grads, lengths=lengths)


def member_table(row_lengths, tok):
    ends = jnp.cumsum(row_lengths).astype(jnp.int32)
    position = lax.iota(jnp.int32, tok)
    seg_of = lax.optimization_barrier(jnp.sum((position[:, None] >= ends[None, :]).astype(jnp.int32), axis=1))
    slots = lax.iota(jnp.int32, row_lengths.shape[0])
    return (seg_of[:, None] == slots[None, :]).astype(jnp.float32)

def seq_sums(product, member):
    carried = jnp.dot(product, member, precision=lax.Precision.HIGHEST)
    return lax.optimization_barrier(jnp.sum(carried * member, axis=0))

def reference(acts, out_grads, lengths):
    blocks = lengths.shape[0]
    tok = acts.shape[0] // blocks
    xb = acts.reshape(blocks, tok, acts.shape[1])
    gb = out_grads.reshape(blocks, tok, out_grads.shape[1])
    bound = math.sqrt(D * FFW * MOST) / 2.0
    contract = (((1,), (1,)), ((), ()))

    def per_block(items):
        x_rows, g_rows, row_lengths = items
        member = member_table(row_lengths, tok)
        act_gram = lax.dot_general(x_rows, x_rows, contract, preferred_element_type=jnp.float32)
        grad_gram = lax.dot_general(g_rows, g_rows, contract, preferred_element_type=jnp.float32)
        norms = jnp.sqrt(seq_sums(act_gram * grad_gram, member))
        factor = jnp.minimum(1.0, bound / (norms + 1e-06))
        token_factor = lax.optimization_barrier(jnp.sum(member * factor[None, :], axis=1))
        return (norms, token_factor)
    seq_norms, token_factor = lax.map(per_block, (xb, gb, lengths))
    weighted = (token_factor.reshape(-1)[:, None] * out_grads.astype(jnp.float32)).astype(jnp.bfloat16)
    total = lax.dot_general(acts, weighted, (((0,), (0,)), ((), ())), preferred_element_type=jnp.float32)
    return (total / SEQS, seq_norms)
```

```python
import math

import jax
import jax.numpy as jnp
from jax import lax
from jax.sharding import PartitionSpec as P

D = 2304
FFW = 18432
MOST = 256

TO_INNER = [(0, 1), (3, 2)]
ACROSS = [(1, 2), (2, 1)]
TO_OUTER = [(1, 0), (2, 3)]
WIDTHS = (512, 512, 512, 512, 512, 512, 512, 512, 256, 256)


def bound():
    return math.sqrt(D * FFW * MOST) / 2.0


def self_gram(rows):
    return lax.dot_general(rows, rows, (((1,), (1,)), ((), ())), preferred_element_type=jnp.float32)


def outer_rows(left, right):
    return lax.dot_general(
        left, right, (((0,), (0,)), ((), ())), preferred_element_type=jnp.float32
    )


def norms_and_factors(acts, out_grads, row_lengths):
    tok = acts.shape[0]
    ends = jnp.cumsum(row_lengths)
    position = lax.iota(jnp.int32, tok)
    seg_of = jnp.sum((position[:, None] >= ends[None, :]).astype(jnp.int32), axis=1)
    slots = lax.iota(jnp.int32, row_lengths.shape[0])
    member = (seg_of[:, None] == slots[None, :]).astype(jnp.float32)
    product = self_gram(acts) * self_gram(out_grads)
    per_token = jnp.sum(jnp.where(seg_of[:, None] == seg_of[None, :], product, 0.0), axis=1)
    squared = lax.psum(jnp.sum(per_token[:, None] * member, axis=0), "mp")
    norms = jnp.sqrt(squared)
    factor = jnp.minimum(1.0, bound() / (norms + 1e-06))
    return norms, jnp.sum(member * factor[None, :], axis=1)


def weigh(token_factor, rows):
    return (token_factor[:, None] * rows.astype(jnp.float32)).astype(jnp.bfloat16)


def by_gathering(acts, out_grads, lengths):
    blocks = lax.axis_size("dp")
    norms, token_factor = norms_and_factors(acts, out_grads, lengths[0])
    rows = lax.all_gather(weigh(token_factor, out_grads), "dp", axis=0, tiled=True)
    mine = lax.all_to_all(acts, "dp", split_axis=1, concat_axis=0, tiled=True)
    return (outer_rows(mine, rows) / (lengths.shape[1] * blocks), norms[None, :])


def on_line_of_four(acts, out_grads, lengths):
    tok, width = acts.shape[0], acts.shape[1] // 4
    z = lax.axis_index("dp")
    side = z // 2
    near = 3 * side
    norms, token_factor = norms_and_factors(acts, out_grads, lengths[0])
    factors = lax.all_gather(token_factor, "dp", axis=0)

    def factor_of(block):
        return lax.dynamic_index_in_dim(factors, block, 0, keepdims=False)

    share = tok // lax.axis_size("mp")
    part = lax.dynamic_slice_in_dim(acts, lax.axis_index("mp") * share, share, axis=0)
    other_half = lax.dynamic_slice_in_dim(part, (1 - side) * 2 * width, 2 * width, axis=1)
    inner_rows = lax.dynamic_slice_in_dim(part, (1 + side) * width, width, axis=1)
    a_across = lax.ppermute(other_half, "dp", ACROSS)
    a_near = lax.ppermute(jnp.concatenate([other_half, inner_rows], axis=1), "dp", TO_INNER)
    a_far = lax.ppermute(a_near[:, : 2 * width], "dp", ACROSS)
    met = lax.all_gather(
        jnp.concatenate([a_across, a_far, a_near[:, 2 * width :]], axis=1), "mp", axis=0, tiled=True
    )

    def columns(array, start):
        return lax.dynamic_slice_in_dim(array, start * width, width, axis=1)

    mine, theirs = 1 - side, side
    left_mine = jnp.concatenate(
        [columns(acts, z), columns(met, mine), columns(met, 2 + mine), met[:, 4 * width :]], axis=0
    )
    left_theirs = jnp.concatenate(
        [columns(acts, near), columns(met, theirs), columns(met, 2 + theirs)], axis=0
    )
    f_own, f_across, f_far, f_near = (
        token_factor, factor_of(3 - z), factor_of(3 - near), factor_of(near)
    )

    total = jnp.zeros((width, out_grads.shape[1]), jnp.float32)
    at = 0
    for c in WIDTHS:
        own = out_grads[:, at : at + c]
        g_near = lax.ppermute(own, "dp", TO_INNER)
        g_across = lax.ppermute(own, "dp", ACROSS)
        g_far = lax.ppermute(g_near, "dp", ACROSS)
        right = jnp.concatenate(
            [weigh(f_own, own), weigh(f_across, g_across), weigh(f_far, g_far), weigh(f_near, g_near)],
            axis=0,
        )
        sent = outer_rows(left_theirs, right[: 3 * tok]).astype(jnp.bfloat16)
        got = lax.ppermute(sent, "dp", TO_OUTER)
        here = outer_rows(left_mine, right) + got.astype(jnp.float32)
        total = lax.dynamic_update_slice_in_dim(total, here / (4 * lengths.shape[1]), at, axis=1)
        at += c
    return (total, norms[None, :])


def solution(mesh):
    in_specs = (P(("groups", "dp"), None), P(("groups", "dp"), "mp"), P(("groups", "dp"), None))
    out_specs = (P(("groups", "dp"), "mp"), P(("groups", "dp"), None))
    on_device = on_line_of_four if mesh.shape["dp"] == 4 else by_gathering
    return jax.shard_map(
        on_device, mesh=mesh, in_specs=in_specs, out_specs=out_specs, check_vma=False
    )
```

```python
import math

import jax
import jax.numpy as jnp
from jax import lax
from jax.experimental import pallas as pl
from jax.experimental.pallas import tpu as pltpu
from jax.sharding import PartitionSpec as P

D = 2304
FFW = 18432
MOST = 256

TO_INNER = [(0, 1), (3, 2)]
ACROSS = [(1, 2), (2, 1)]
TO_OUTER = [(1, 0), (2, 3)]
WIDTHS = (768,768,768,768,768,512,256)
LATE = 1
SENT, GOT, DONE = 4,6,7

COST = pl.CostEstimate(flops=0, bytes_accessed=0, transcendentals=0)


def bound():
    return math.sqrt(D * FFW * MOST) / 2.0


def self_gram(rows):
    return lax.dot_general(rows, rows, (((1,), (1,)), ((), ())), preferred_element_type=jnp.float32)


def outer_rows(left, right):
    return lax.dot_general(
        left, right, (((0,), (0,)), ((), ())), preferred_element_type=jnp.float32
    )


def norms_and_factors(acts, out_grads, row_lengths, *others):
    tok = acts.shape[0]
    ends = jnp.cumsum(row_lengths)
    position = lax.iota(jnp.int32, tok)
    seg_of = jnp.sum((position[:, None] >= ends[None, :]).astype(jnp.int32), axis=1)
    slots = lax.iota(jnp.int32, row_lengths.shape[0])
    member = (seg_of[:, None] == slots[None, :]).astype(jnp.float32)
    product = self_gram(acts) * self_gram(out_grads)
    per_token = jnp.sum(jnp.where(seg_of[:, None] == seg_of[None, :], product, 0.0), axis=1)
    squared = lax.psum(after(jnp.sum(per_token[:, None] * member, axis=0), others), "mp")
    norms = jnp.sqrt(squared)
    factor = jnp.minimum(1.0, bound() / (norms + 1e-06))
    return norms, jnp.sum(member * factor[None, :], axis=1)


def after(array, *others):
    return lax.optimization_barrier((array, *(o for some in others for o in some)))[0]


def weigh(token_factor, rows):
    return (token_factor[:, None] * rows.astype(jnp.float32)).astype(jnp.bfloat16)


def tile_of(start, width):
    return 256 if start % 256 == 0 and width % 256 == 0 else 128


def block_sum(left_ref, rows_refs):
    tok = rows_refs[0].shape[0]
    total = None
    for i, rows_ref in enumerate(rows_refs):
        term = jnp.dot(left_ref[:, i * tok : (i + 1) * tok], rows_ref[...], preferred_element_type=jnp.float32)
        total = term if total is None else total + term
    return total


def whole(array):
    return pl.BlockSpec(array.shape, lambda i: (0, 0))


def sum_for_outer(left, *rows):
    def kernel(left_ref, *refs):
        refs[-1][...] = block_sum(left_ref, refs[:-1]).astype(jnp.bfloat16)

    tok, width = rows[0].shape
    tile = tile_of(0, width)
    return pl.pallas_call(
        kernel,
        grid=(width // tile,),
        out_shape=jax.ShapeDtypeStruct((left.shape[0], width), jnp.bfloat16),
        in_specs=[whole(left)] + [pl.BlockSpec((tok, tile), lambda i: (0, i))] * len(rows),
        out_specs=pl.BlockSpec((left.shape[0], tile), lambda i: (0, i)),
        compiler_params=pltpu.CompilerParams(vmem_limit_bytes=32 << 20),
        cost_estimate=COST,
        name="sum_for_outer",
    )(left, *rows)


def own_rows(left, rows, got, total, mark, start, columns, share):
    tok, width = rows[0].shape
    tile = tile_of(start, width)
    before = [] if total is None else [total, mark]

    def kernel(left_ref, *refs):
        here = block_sum(left_ref, refs[:4])
        refs[-2][...] = (here + refs[4][...].astype(jnp.float32)) * (1.0 / share)
        refs[-1][...] = jnp.zeros(refs[-1].shape, jnp.float32)

    return pl.pallas_call(
        kernel,
        grid=(width // tile,),
        out_shape=[
            jax.ShapeDtypeStruct((left.shape[0], columns), jnp.float32),
            jax.ShapeDtypeStruct((8, 128), jnp.float32),
        ],
        in_specs=[whole(left)]
        + [pl.BlockSpec((tok, tile), lambda i: (0, i))] * 4
        + [pl.BlockSpec((left.shape[0], tile), lambda i: (0, i))]
        + [pl.BlockSpec(memory_space=pl.ANY)] * len(before),
        out_specs=[
            pl.BlockSpec((left.shape[0], tile), lambda i: (0, start // tile + i)),
            pl.BlockSpec((8, 128), lambda i: (0, 0)),
        ],
        input_output_aliases={6: 0} if before else {},
        compiler_params=pltpu.CompilerParams(vmem_limit_bytes=32 << 20),
        cost_estimate=COST,
        name="own_rows",
    )(left, *rows, got, *before)


def by_gathering(acts, out_grads, lengths):
    blocks = lax.axis_size("dp")
    norms, token_factor = norms_and_factors(acts, out_grads, lengths[0])
    rows = lax.all_gather(weigh(token_factor, out_grads), "dp", axis=0, tiled=True)
    mine = lax.all_to_all(acts, "dp", split_axis=1, concat_axis=0, tiled=True)
    return (outer_rows(mine, rows) / (lengths.shape[1] * blocks), norms[None, :])


def on_line_of_four(acts, out_grads, lengths):
    tok, width = acts.shape[0], acts.shape[1] // 4
    z = lax.axis_index("dp")
    side = z // 2
    outer = 3 * side
    share = tok // lax.axis_size("mp")
    part = lax.dynamic_slice_in_dim(acts, lax.axis_index("mp") * share, share, axis=0)
    other_half = lax.dynamic_slice_in_dim(part, (1 - side) * 2 * width, 2 * width, axis=1)
    inner_rows = lax.dynamic_slice_in_dim(part, (1 + side) * width, width, axis=1)

    chunks = len(WIDTHS)
    starts = [sum(WIDTHS[:j]) for j in range(chunks)]
    own, near, across, far, got = ({} for _ in range(5))

    crossed = []
    due = [[] for _ in range(2 * chunks + 24)]

    def cross(array):
        at = len(crossed)
        crossed.append(lax.ppermute(after(array, crossed[-2:-1], due[at]), "dp", ACROSS))
        return crossed[-1]

    def bring(j):
        at = len(crossed)
        own[j] = (weighted if j else weigh(f_own, out_grads))[:, starts[j] : starts[j] + WIDTHS[j]]
        across[j] = cross(own[j])
        near[j] = lax.ppermute(after(own[j], crossed[-3:-2]), "dp", TO_INNER)

    def columns(array, start):
        return lax.dynamic_slice_in_dim(array, start * width, width, axis=1)

    a_relayed = lax.ppermute(other_half, "dp", TO_INNER)
    a_across = cross(other_half)
    norms, f_own = norms_and_factors(acts, out_grads, lengths[0], [a_relayed])
    a_near = lax.ppermute(after(inner_rows, [a_relayed]), "dp", TO_INNER)
    a_far = cross(a_relayed)
    met = lax.all_gather(
        jnp.concatenate([after(a_across, [f_own]), a_far, a_near], axis=1), "mp", axis=0, tiled=True
    )
    mine, theirs = 1 - side, side
    left_mine = jnp.concatenate(
        [columns(acts, z), columns(met, mine), columns(met, 2 + mine), met[:, 4 * width :]], axis=0
    ).T
    left_theirs = jnp.concatenate(
        [columns(acts, outer), columns(met, theirs), columns(met, 2 + theirs)], axis=0
    ).T

    bring(0)
    weighted = weigh(f_own, after(out_grads, [f_own]))
    bring(1)
    total = mark = None
    for j in range(chunks):
        at = len(crossed)
        far[j] = cross(near[j])
        if j + 2 < chunks:
            bring(j + 2)
        sent = sum_for_outer(left_theirs, own[j], across[j], far[j])
        got[j] = lax.ppermute(after(sent, [got[j - 1]] if j else []), "dp", TO_OUTER)
        total, mark = own_rows(
            left_mine, (own[j], across[j], far[j], near[j]), got[j], total, mark, starts[j], out_grads.shape[1],
            4 * lengths.shape[1],
        )
        late = max(0, 2 - j) * LATE
        due[at + SENT + late] += [sent]
        due[at + GOT + late] += [got[j]]
        due[at + DONE + late] += [mark]
    return (total, norms[None, :])


def solution(mesh):
    in_specs = (P(("groups", "dp"), None), P(("groups", "dp"), "mp"), P(("groups", "dp"), None))
    out_specs = (P(("groups", "dp"), "mp"), P(("groups", "dp"), None))
    on_device = on_line_of_four if mesh.shape["dp"] == 4 else by_gathering
    return jax.shard_map(
        on_device, mesh=mesh, in_specs=in_specs, out_specs=out_specs, check_vma=False
    )
```

```python
import math

import jax
import jax.numpy as jnp
from jax import lax
from jax.experimental import pallas as pl
from jax.experimental.pallas import tpu as pltpu
from jax.sharding import PartitionSpec as P

D = 2304
FFW = 18432
MOST = 256

TO_INNER = [(0, 1), (3, 2)]
ACROSS = [(1, 2), (2, 1)]
TO_OUTER = [(1, 0), (2, 3)]
WIDTHS = (768,768,768,768,768,768)
LAST = (768,)
LAST_WAITS = (2,2)
END = 99
LATE = 1
SENT, GOT, DONE = 4,6,4

COST = pl.CostEstimate(flops=0, bytes_accessed=0, transcendentals=0)


def bound():
    return math.sqrt(D * FFW * MOST) / 2.0


def outer_rows(left, right):
    return lax.dot_general(
        left, right, (((0,), (0,)), ((), ())), preferred_element_type=jnp.float32
    )


def gram_steps(acts, out_grads):
    for steps in (3, 2, 1):
        if acts.shape[1] % (steps * 128) == 0 and out_grads.shape[1] % (steps * 128) == 0:
            return steps
    return 1


def squared_norms(acts, out_grads, lengths):
    tok, segments = acts.shape[0], lengths.shape[1]
    steps = gram_steps(acts, out_grads)

    def kernel(lengths_ref, acts_ref, grads_ref, out_ref, act_gram, grad_gram):
        step = pl.program_id(0)

        @pl.when(step == 0)
        def _():
            act_gram[...] = jnp.zeros_like(act_gram)
            grad_gram[...] = jnp.zeros_like(grad_gram)

        contract = (((1,), (1,)), ((), ()))
        act_gram[...] += lax.dot_general(
            acts_ref[...], acts_ref[...], contract, preferred_element_type=jnp.float32
        )
        grad_gram[...] += lax.dot_general(
            grads_ref[...], grads_ref[...], contract, preferred_element_type=jnp.float32
        )

        @pl.when(step == steps - 1)
        def _():
            of_row = jnp.zeros((tok, 1), jnp.int32)
            of_column = jnp.zeros((1, tok), jnp.int32)
            end = 0
            for j in range(segments):
                end += lengths_ref[0, j]
                of_row += (lax.broadcasted_iota(jnp.int32, (tok, 1), 0) >= end).astype(jnp.int32)
                of_column += (lax.broadcasted_iota(jnp.int32, (1, tok), 1) >= end).astype(jnp.int32)
            product = jnp.where(of_row == of_column, act_gram[...] * grad_gram[...], 0.0)
            per_token = jnp.sum(product, axis=1, keepdims=True)
            lane = lax.broadcasted_iota(jnp.int32, (1, 128), 1)
            out_ref[...] = jnp.sum(jnp.where(of_row == lane, per_token, 0.0), axis=0, keepdims=True)

    return pl.pallas_call(
        kernel,
        grid=(steps,),
        out_shape=jax.ShapeDtypeStruct((1, 128), jnp.float32),
        in_specs=[
            pl.BlockSpec(memory_space=pltpu.SMEM),
            pl.BlockSpec((tok, acts.shape[1] // steps), lambda i: (0, i)),
            pl.BlockSpec((tok, out_grads.shape[1] // steps), lambda i: (0, i)),
        ],
        out_specs=pl.BlockSpec((1, 128), lambda i: (0, 0)),
        scratch_shapes=[pltpu.VMEM((tok, tok), jnp.float32)] * 2,
        compiler_params=pltpu.CompilerParams(vmem_limit_bytes=32 << 20),
        cost_estimate=pl.CostEstimate(
            flops=2 * tok * (acts.size + out_grads.size),
            bytes_accessed=2 * (acts.size + out_grads.size),
            transcendentals=0,
        ),
        name="squared_norms",
    )(lengths, acts, out_grads)


def norms_and_factors(acts, out_grads, lengths, *others):
    tok, segments = acts.shape[0], lengths.shape[1]
    ends = jnp.cumsum(lengths[0])
    position = lax.iota(jnp.int32, tok)
    seg_of = jnp.sum((position[:, None] >= ends[None, :]).astype(jnp.int32), axis=1)
    member = (seg_of[:, None] == lax.iota(jnp.int32, segments)[None, :]).astype(jnp.float32)
    squared = lax.psum(after(squared_norms(acts, out_grads, lengths), others), "mp")
    norms = jnp.sqrt(squared[0, :segments])
    factor = jnp.minimum(1.0, bound() / (norms + 1e-06))
    return norms, jnp.sum(member * factor[None, :], axis=1)


def after(array, *others):
    return lax.optimization_barrier((array, *(o for some in others for o in some)))[0]


def weigh(token_factor, rows):
    return (token_factor[:, None] * rows.astype(jnp.float32)).astype(jnp.bfloat16)


def tile_of(start, width):
    return 256 if start % 256 == 0 and width % 256 == 0 else 128


def block_sum(left_ref, rows_refs):
    tok = rows_refs[0].shape[0]
    total = None
    for i, rows_ref in enumerate(rows_refs):
        term = jnp.dot(left_ref[:, i * tok : (i + 1) * tok], rows_ref[...], preferred_element_type=jnp.float32)
        total = term if total is None else total + term
    return total


def whole(array):
    return pl.BlockSpec(array.shape, lambda i: (0, 0))


def tiles_of(array, width, place, tile):
    first = 0 if array.shape[1] == width else place // tile
    return pl.BlockSpec((array.shape[0], tile), lambda i: (0, first + i))


def sum_for_outer(left, place, *rows):
    def kernel(left_ref, *refs):
        refs[-1][...] = block_sum(left_ref, refs[:-1]).astype(jnp.bfloat16)

    tok, width = rows[-1].shape
    tile = tile_of(place, width)
    return pl.pallas_call(
        kernel,
        grid=(width // tile,),
        out_shape=jax.ShapeDtypeStruct((left.shape[0], width), jnp.bfloat16),
        in_specs=[whole(left)] + [tiles_of(array, width, place, tile) for array in rows],
        out_specs=pl.BlockSpec((left.shape[0], tile), lambda i: (0, i)),
        compiler_params=pltpu.CompilerParams(vmem_limit_bytes=32 << 20),
        cost_estimate=COST,
        name="sum_for_outer",
    )(left, *rows)


def own_rows(left, place, rows, got, total, mark, start, columns, share):
    width = got.shape[1]
    tile = min(tile_of(start, width), tile_of(place, width))
    before = [] if total is None else [total, mark]

    def kernel(left_ref, *refs):
        here = block_sum(left_ref, refs[:4])
        refs[-2][...] = (here + refs[4][...].astype(jnp.float32)) * (1.0 / share)
        refs[-1][...] = jnp.zeros(refs[-1].shape, jnp.float32)

    return pl.pallas_call(
        kernel,
        grid=(width // tile,),
        out_shape=[
            jax.ShapeDtypeStruct((left.shape[0], columns), jnp.float32),
            jax.ShapeDtypeStruct((8, 128), jnp.float32),
        ],
        in_specs=[whole(left)]
        + [tiles_of(array, width, place, tile) for array in (*rows, got)]
        + [pl.BlockSpec(memory_space=pl.ANY)] * len(before),
        out_specs=[
            pl.BlockSpec((left.shape[0], tile), lambda i: (0, start // tile + i)),
            pl.BlockSpec((8, 128), lambda i: (0, 0)),
        ],
        input_output_aliases={6: 0} if before else {},
        compiler_params=pltpu.CompilerParams(vmem_limit_bytes=32 << 20),
        cost_estimate=COST,
        name="own_rows",
    )(left, *rows, got, *before)


def by_gathering(acts, out_grads, lengths):
    blocks = lax.axis_size("dp")
    norms, token_factor = norms_and_factors(acts, out_grads, lengths)
    rows = lax.all_gather(weigh(token_factor, out_grads), "dp", axis=0, tiled=True)
    mine = lax.all_to_all(acts, "dp", split_axis=1, concat_axis=0, tiled=True)
    return (outer_rows(mine, rows) / (lengths.shape[1] * blocks), norms[None, :])


def on_line_of_four(acts, out_grads, lengths):
    tok, width = acts.shape[0], acts.shape[1] // 4
    z = lax.axis_index("dp")
    side = z // 2
    outer = 3 * side
    share = tok // lax.axis_size("mp")
    part = lax.dynamic_slice_in_dim(acts, lax.axis_index("mp") * share, share, axis=0)
    other_half = lax.dynamic_slice_in_dim(part, (1 - side) * 2 * width, 2 * width, axis=1)
    inner_rows = lax.dynamic_slice_in_dim(part, (1 + side) * width, width, axis=1)

    starts = [sum(WIDTHS[:j]) for j in range(len(WIDTHS))]
    pieces = [(j, 0, width) for j, width in enumerate(WIDTHS[:-1])]
    pieces += [(len(WIDTHS) - 1, sum(LAST[:i]), width) for i, width in enumerate(LAST)]
    own, across = {}, {}

    crossed = []
    due = [[] for _ in range(2 * len(pieces) + 24)]

    def cross(array, before=2):
        at = len(crossed)
        crossed.append(lax.ppermute(after(array, crossed[at - before : at - before + 1], due[at]), "dp", ACROSS))
        return crossed[-1]

    def bring(j):
        own[j] = (weighted if j else weigh(f_own, out_grads))[:, starts[j] : starts[j] + WIDTHS[j]]
        across[j] = cross(own[j])

    def from_outside(j, place, width):
        rows = own[j]
        if width < WIDTHS[j]:
            rows = weighted[:, starts[j] + place : starts[j] + place + width]
        return lax.ppermute(after(rows, crossed[-3:-2]), "dp", TO_INNER)

    def columns(array, start):
        return lax.dynamic_slice_in_dim(array, start * width, width, axis=1)

    a_relayed = lax.ppermute(other_half, "dp", TO_INNER)
    a_across = cross(other_half)
    norms, f_own = norms_and_factors(acts, out_grads, lengths, [a_relayed])
    a_near = lax.ppermute(after(inner_rows, [a_relayed]), "dp", TO_INNER)
    a_far = cross(a_relayed)
    met = lax.all_gather(
        jnp.concatenate([after(a_across, [f_own]), a_far, a_near], axis=1), "mp", axis=0, tiled=True
    )
    mine, theirs = 1 - side, side
    left_mine = jnp.concatenate(
        [columns(acts, z), columns(met, mine), columns(met, 2 + mine), met[:, 4 * width :]], axis=0
    ).T
    left_theirs = jnp.concatenate(
        [columns(acts, outer), columns(met, theirs), columns(met, 2 + theirs)], axis=0
    ).T

    bring(0)
    near = [from_outside(*pieces[0])]
    weighted = weigh(f_own, after(out_grads, [f_own]))
    bring(1)
    near += [from_outside(*piece) for piece in pieces[1:] if piece[0] == 1]
    total = mark = None
    gots = []
    for i, (j, place, width) in enumerate(pieces):
        at = len(crossed)
        last = j == len(WIDTHS) - 1
        far = cross(near[i], 2 if not last or i == len(pieces) - 1 and len(LAST) > 2 else LAST_WAITS[place > 0])
        if j + 2 < len(WIDTHS):
            bring(j + 2)
            near += [from_outside(*piece) for piece in pieces if piece[0] == j + 2]
        sent = sum_for_outer(left_theirs, place, own[j], across[j], far)
        got = lax.ppermute(after(sent, gots[-1:]), "dp", TO_OUTER)
        gots.append(got)
        total, mark = own_rows(
            left_mine, place, (own[j], across[j], far, near[i]), got, total, mark, starts[j] + place,
            out_grads.shape[1], 4 * lengths.shape[1],
        )
        late = max(0, 2 - j) * LATE
        for later, array in ((SENT, sent), (GOT, got), (DONE, mark)):
            if at + later + late <= 2 * len(WIDTHS) + END:
                due[at + later + late] += [array]
    return (total, norms[None, :])


def solution(mesh):
    in_specs = (P(("groups", "dp"), None), P(("groups", "dp"), "mp"), P(("groups", "dp"), None))
    out_specs = (P(("groups", "dp"), "mp"), P(("groups", "dp"), None))
    on_device = on_line_of_four if mesh.shape["dp"] == 4 else by_gathering
    return jax.shard_map(
        on_device, mesh=mesh, in_specs=in_specs, out_specs=out_specs, check_vma=False
    )
```

```python
import math

import jax
import jax.numpy as jnp
from jax import lax
from jax.experimental import pallas as pl
from jax.experimental.pallas import tpu as pltpu
from jax.sharding import PartitionSpec as P

D = 2304
FFW = 18432
MOST = 256

TO_INNER = [(0, 1), (3, 2)]
ACROSS = [(1, 2), (2, 1)]
TO_OUTER = [(1, 0), (2, 3)]
WIDTHS = (1024,768,768,768,768,512)
LAST = (512,)
LAST_WAITS = (1,1)
END = 99
LATE = 1
SENT, GOT, DONE = 4,6,4

COST = pl.CostEstimate(flops=0, bytes_accessed=0, transcendentals=0)


def bound():
    return math.sqrt(D * FFW * MOST) / 2.0


def outer_rows(left, right):
    return lax.dot_general(
        left, right, (((0,), (0,)), ((), ())), preferred_element_type=jnp.float32
    )


def gram_steps(acts, out_grads):
    for steps in (3, 2, 1):
        if acts.shape[1] % (steps * 128) == 0 and out_grads.shape[1] % (steps * 128) == 0:
            return steps
    return 1


def squared_norms(acts, out_grads, lengths):
    tok, segments = acts.shape[0], lengths.shape[1]
    steps = gram_steps(acts, out_grads)
    half = tok // 2
    quarters = ((0, 0), (half, 0), (half, half))

    def kernel(lengths_ref, acts_ref, grads_ref, out_ref, member_ref, act_gram, grad_gram):
        step = pl.program_id(0)

        @pl.when(step == 0)
        def _():
            act_gram[...] = jnp.zeros_like(act_gram)
            grad_gram[...] = jnp.zeros_like(grad_gram)

        for rows_ref, gram in ((acts_ref, act_gram), (grads_ref, grad_gram)):
            rows = rows_ref[...]
            for top, left in quarters:
                gram[top : top + half, left : left + half] += lax.dot_general(
                    rows[top : top + half],
                    rows[left : left + half],
                    (((1,), (1,)), ((), ())),
                    preferred_element_type=jnp.float32,
                )

        @pl.when(step == steps - 1)
        def _():
            squared = jnp.zeros((1, 128), jnp.float32)
            lane = lax.broadcasted_iota(jnp.int32, (1, 128), 1)
            for top, left in quarters:
                of_row = jnp.zeros((half, 1), jnp.int32)
                of_column = jnp.zeros((1, half), jnp.int32)
                end = 0
                for j in range(segments):
                    end += lengths_ref[0, j]
                    of_row += (top + lax.broadcasted_iota(jnp.int32, (half, 1), 0) >= end).astype(jnp.int32)
                    of_column += (left + lax.broadcasted_iota(jnp.int32, (1, half), 1) >= end).astype(jnp.int32)
                place = (slice(top, top + half), slice(left, left + half))
                product = jnp.where(of_row == of_column, act_gram[place] * grad_gram[place], 0.0)
                per_token = jnp.sum(product, axis=1, keepdims=True) * (1.0 if top == left else 2.0)
                squared += jnp.sum(jnp.where(of_row == lane, per_token, 0.0), axis=0, keepdims=True)
                if top == left:
                    member_ref[top : top + half] = (of_row == lane).astype(jnp.float32)
            out_ref[...] = squared

    return pl.pallas_call(
        kernel,
        grid=(steps,),
        out_shape=[jax.ShapeDtypeStruct((1, 128), jnp.float32), jax.ShapeDtypeStruct((tok, 128), jnp.float32)],
        in_specs=[
            pl.BlockSpec(memory_space=pltpu.SMEM),
            pl.BlockSpec((tok, acts.shape[1] // steps), lambda i: (0, i)),
            pl.BlockSpec((tok, out_grads.shape[1] // steps), lambda i: (0, i)),
        ],
        out_specs=[pl.BlockSpec((1, 128), lambda i: (0, 0)), pl.BlockSpec((tok, 128), lambda i: (0, 0))],
        scratch_shapes=[pltpu.VMEM((tok, tok), jnp.float32)] * 2,
        compiler_params=pltpu.CompilerParams(vmem_limit_bytes=56 << 20),
        cost_estimate=pl.CostEstimate(
            flops=2 * tok * (acts.size + out_grads.size),
            bytes_accessed=2 * (acts.size + out_grads.size),
            transcendentals=0,
        ),
        name="squared_norms",
    )(lengths, acts, out_grads)


def norms_and_factors(acts, out_grads, lengths, *others):
    squared, member = squared_norms(acts, out_grads, lengths)
    norms = jnp.sqrt(lax.psum(after(squared, others), "mp"))
    factor = jnp.minimum(1.0, bound() / (norms + 1e-06))
    return norms[0, : lengths.shape[1]], jnp.sum(member * factor, axis=1)


def after(array, *others):
    return lax.optimization_barrier((array, *(o for some in others for o in some)))[0]


def weigh(token_factor, rows):
    return (token_factor[:, None] * rows.astype(jnp.float32)).astype(jnp.bfloat16)


def tile_of(start, width):
    return 256 if start % 256 == 0 and width % 256 == 0 else 128


def block_sum(left_ref, rows_refs):
    tok = rows_refs[0].shape[0]
    total = None
    for i, rows_ref in enumerate(rows_refs):
        term = jnp.dot(left_ref[:, i * tok : (i + 1) * tok], rows_ref[...], preferred_element_type=jnp.float32)
        total = term if total is None else total + term
    return total


def whole(array):
    return pl.BlockSpec(array.shape, lambda i: (0, 0))


def tiles_of(array, width, place, tile):
    first = 0 if array.shape[1] == width else place // tile
    return pl.BlockSpec((array.shape[0], tile), lambda i: (0, first + i))


def sum_for_outer(left, place, *rows):
    def kernel(left_ref, *refs):
        refs[-1][...] = block_sum(left_ref, refs[:-1]).astype(jnp.bfloat16)

    tok, width = rows[-1].shape
    tile = tile_of(place, width)
    return pl.pallas_call(
        kernel,
        grid=(width // tile,),
        out_shape=jax.ShapeDtypeStruct((left.shape[0], width), jnp.bfloat16),
        in_specs=[whole(left)] + [tiles_of(array, width, place, tile) for array in rows],
        out_specs=pl.BlockSpec((left.shape[0], tile), lambda i: (0, i)),
        compiler_params=pltpu.CompilerParams(vmem_limit_bytes=32 << 20),
        cost_estimate=COST,
        name="sum_for_outer",
    )(left, *rows)


def own_rows(left, place, rows, got, total, mark, start, columns, share):
    width = got.shape[1]
    tile = min(tile_of(start, width), tile_of(place, width))
    before = [] if total is None else [total, mark]

    def kernel(left_ref, *refs):
        here = block_sum(left_ref, refs[:4])
        refs[-2][...] = (here + refs[4][...].astype(jnp.float32)) * (1.0 / share)
        refs[-1][...] = jnp.zeros(refs[-1].shape, jnp.float32)

    return pl.pallas_call(
        kernel,
        grid=(width // tile,),
        out_shape=[
            jax.ShapeDtypeStruct((left.shape[0], columns), jnp.float32),
            jax.ShapeDtypeStruct((8, 128), jnp.float32),
        ],
        in_specs=[whole(left)]
        + [tiles_of(array, width, place, tile) for array in (*rows, got)]
        + [pl.BlockSpec(memory_space=pl.ANY)] * len(before),
        out_specs=[
            pl.BlockSpec((left.shape[0], tile), lambda i: (0, start // tile + i)),
            pl.BlockSpec((8, 128), lambda i: (0, 0)),
        ],
        input_output_aliases={6: 0} if before else {},
        compiler_params=pltpu.CompilerParams(vmem_limit_bytes=32 << 20),
        cost_estimate=COST,
        name="own_rows",
    )(left, *rows, got, *before)


def by_gathering(acts, out_grads, lengths):
    blocks = lax.axis_size("dp")
    norms, token_factor = norms_and_factors(acts, out_grads, lengths)
    rows = lax.all_gather(weigh(token_factor, out_grads), "dp", axis=0, tiled=True)
    mine = lax.all_to_all(acts, "dp", split_axis=1, concat_axis=0, tiled=True)
    return (outer_rows(mine, rows) / (lengths.shape[1] * blocks), norms[None, :])


def on_line_of_four(acts, out_grads, lengths):
    tok, width = acts.shape[0], acts.shape[1] // 4
    z = lax.axis_index("dp")
    side = z // 2
    outer = 3 * side
    share = tok // lax.axis_size("mp")
    part = lax.dynamic_slice_in_dim(acts, lax.axis_index("mp") * share, share, axis=0)
    other_half = lax.dynamic_slice_in_dim(part, (1 - side) * 2 * width, 2 * width, axis=1)
    inner_rows = lax.dynamic_slice_in_dim(part, (1 + side) * width, width, axis=1)

    starts = [sum(WIDTHS[:j]) for j in range(len(WIDTHS))]
    pieces = [(j, 0, width) for j, width in enumerate(WIDTHS[:-1])]
    pieces += [(len(WIDTHS) - 1, sum(LAST[:i]), width) for i, width in enumerate(LAST)]
    own, across = {}, {}

    crossed = []
    due = [[] for _ in range(2 * len(pieces) + 24)]

    def cross(array, before=2):
        at = len(crossed)
        crossed.append(lax.ppermute(after(array, crossed[at - before : at - before + 1], due[at]), "dp", ACROSS))
        return crossed[-1]

    def bring(j):
        own[j] = (weighted if j else weigh(f_own, out_grads))[:, starts[j] : starts[j] + WIDTHS[j]]
        across[j] = cross(own[j])

    def from_outside(j, place, width):
        rows = own[j]
        if width < WIDTHS[j]:
            rows = weighted[:, starts[j] + place : starts[j] + place + width]
        return lax.ppermute(after(rows, crossed[-3:-2]), "dp", TO_INNER)

    def columns(array, start):
        return lax.dynamic_slice_in_dim(array, start * width, width, axis=1)

    a_relayed = lax.ppermute(other_half, "dp", TO_INNER)
    a_across = cross(other_half)
    norms, f_own = norms_and_factors(acts, out_grads, lengths, [a_relayed])
    a_near = lax.ppermute(after(inner_rows, [a_relayed]), "dp", TO_INNER)
    a_far = cross(a_relayed)
    met = lax.all_gather(
        jnp.concatenate([after(a_across, [f_own]), a_far, a_near], axis=1), "mp", axis=0, tiled=True
    )
    mine, theirs = 1 - side, side
    left_mine = jnp.concatenate(
        [columns(acts, z), columns(met, mine), columns(met, 2 + mine), met[:, 4 * width :]], axis=0
    ).T
    left_theirs = jnp.concatenate(
        [columns(acts, outer), columns(met, theirs), columns(met, 2 + theirs)], axis=0
    ).T

    bring(0)
    near = [from_outside(*pieces[0])]
    weighted = weigh(f_own, after(out_grads, [f_own]))
    bring(1)
    near += [from_outside(*piece) for piece in pieces[1:] if piece[0] == 1]
    total = mark = None
    gots = []
    for i, (j, place, width) in enumerate(pieces):
        at = len(crossed)
        last = j == len(WIDTHS) - 1
        far = cross(near[i], 2 if not last or i == len(pieces) - 1 and len(LAST) > 2 else LAST_WAITS[place > 0])
        if j + 2 < len(WIDTHS):
            bring(j + 2)
            near += [from_outside(*piece) for piece in pieces if piece[0] == j + 2]
        sent = sum_for_outer(left_theirs, place, own[j], across[j], far)
        got = lax.ppermute(after(sent, gots[-1:]), "dp", TO_OUTER)
        gots.append(got)
        total, mark = own_rows(
            left_mine, place, (own[j], across[j], far, near[i]), got, total, mark, starts[j] + place,
            out_grads.shape[1], 4 * lengths.shape[1],
        )
        late = max(0, 2 - j) * LATE
        for later, array in ((SENT, sent), (GOT, got), (DONE, mark)):
            if at + later + late <= 2 * len(WIDTHS) + END:
                due[at + later + late] += [array]
    return (total, norms[None, :])


def solution(mesh):
    in_specs = (P(("groups", "dp"), None), P(("groups", "dp"), "mp"), P(("groups", "dp"), None))
    out_specs = (P(("groups", "dp"), "mp"), P(("groups", "dp"), None))
    on_device = on_line_of_four if mesh.shape["dp"] == 4 else by_gathering
    return jax.shard_map(
        on_device, mesh=mesh, in_specs=in_specs, out_specs=out_specs, check_vma=False
    )
```

```python
import math

import jax
import jax.numpy as jnp
from jax import lax
from jax.experimental import pallas as pl
from jax.experimental.pallas import tpu as pltpu
from jax.sharding import PartitionSpec as P

D = 2304
FFW = 18432
MOST = 256

TO_INNER = [(0, 1), (3, 2)]
ACROSS = [(1, 2), (2, 1)]
TO_OUTER = [(1, 0), (2, 3)]
WIDTHS = (1024,768,768,768,768,512)
LAST = (512,)
LAST_WAITS = (1,1)
END = 99
LATE = 1
SENT, GOT, DONE = 4,6,4

COST = pl.CostEstimate(flops=0, bytes_accessed=0, transcendentals=0)


def bound():
    return math.sqrt(D * FFW * MOST) / 2.0


def outer_rows(left, right):
    return lax.dot_general(
        left, right, (((0,), (0,)), ((), ())), preferred_element_type=jnp.float32
    )


def gram_steps(acts, out_grads):
    for steps in (2, 1):
        if acts.shape[1] % (steps * 128) == 0 and out_grads.shape[1] % (steps * 128) == 0:
            return steps
    return 1


def squared_norms(acts, out_grads, lengths):
    tok, segments = acts.shape[0], lengths.shape[1]
    steps = gram_steps(acts, out_grads)
    half = tok // 2
    quarters = ((0, 0), (half, 0), (half, half))

    def kernel(lengths_ref, acts_ref, grads_ref, out_ref, member_ref, act_gram, grad_gram):
        step = pl.program_id(0)

        @pl.when(step == 0)
        def _():
            act_gram[...] = jnp.zeros_like(act_gram)
            grad_gram[...] = jnp.zeros_like(grad_gram)

        for rows_ref, gram in ((acts_ref, act_gram), (grads_ref, grad_gram)):
            rows = rows_ref[...]
            for top, left in quarters:
                gram[top : top + half, left : left + half] += lax.dot_general(
                    rows[top : top + half],
                    rows[left : left + half],
                    (((1,), (1,)), ((), ())),
                    preferred_element_type=jnp.float32,
                )

        @pl.when(step == steps - 1)
        def _():
            squared = jnp.zeros((1, 128), jnp.float32)
            lane = lax.broadcasted_iota(jnp.int32, (1, 128), 1)
            for top, left in quarters:
                of_row = jnp.zeros((half, 1), jnp.int32)
                of_column = jnp.zeros((1, half), jnp.int32)
                end = 0
                for j in range(segments):
                    end += lengths_ref[0, j]
                    of_row += (top + lax.broadcasted_iota(jnp.int32, (half, 1), 0) >= end).astype(jnp.int32)
                    of_column += (left + lax.broadcasted_iota(jnp.int32, (1, half), 1) >= end).astype(jnp.int32)
                place = (slice(top, top + half), slice(left, left + half))
                product = jnp.where(of_row == of_column, act_gram[place] * grad_gram[place], 0.0)
                per_token = jnp.sum(product, axis=1, keepdims=True) * (1.0 if top == left else 2.0)
                squared += jnp.sum(jnp.where(of_row == lane, per_token, 0.0), axis=0, keepdims=True)
                if top == left:
                    member_ref[top : top + half] = (of_row == lane).astype(jnp.float32)
            out_ref[...] = squared

    return pl.pallas_call(
        kernel,
        grid=(steps,),
        out_shape=[jax.ShapeDtypeStruct((1, 128), jnp.float32), jax.ShapeDtypeStruct((tok, 128), jnp.float32)],
        in_specs=[
            pl.BlockSpec(memory_space=pltpu.SMEM),
            pl.BlockSpec((tok, acts.shape[1] // steps), lambda i: (0, i)),
            pl.BlockSpec((tok, out_grads.shape[1] // steps), lambda i: (0, i)),
        ],
        out_specs=[pl.BlockSpec((1, 128), lambda i: (0, 0)), pl.BlockSpec((tok, 128), lambda i: (0, 0))],
        scratch_shapes=[pltpu.VMEM((tok, tok), jnp.float32)] * 2,
        compiler_params=pltpu.CompilerParams(vmem_limit_bytes=56 << 20),
        cost_estimate=pl.CostEstimate(
            flops=2 * tok * (acts.size + out_grads.size),
            bytes_accessed=2 * (acts.size + out_grads.size),
            transcendentals=0,
        ),
        name="squared_norms",
    )(lengths, acts, out_grads)


def norms_and_factors(acts, out_grads, lengths, *others):
    squared, member = squared_norms(acts, out_grads, lengths)
    norms = jnp.sqrt(lax.psum(after(squared, others), "mp"))
    factor = jnp.minimum(1.0, bound() / (norms + 1e-06))
    return norms[0, : lengths.shape[1]], jnp.sum(member * factor, axis=1)


def after(array, *others):
    return lax.optimization_barrier((array, *(o for some in others for o in some)))[0]


def weigh(token_factor, rows):
    return (token_factor[:, None] * rows.astype(jnp.float32)).astype(jnp.bfloat16)


def tile_of(start, width):
    return 256 if start % 256 == 0 and width % 256 == 0 else 128


def block_sum(left_ref, rows_refs):
    tok = rows_refs[0].shape[0]
    total = None
    for i, rows_ref in enumerate(rows_refs):
        term = jnp.dot(left_ref[:, i * tok : (i + 1) * tok], rows_ref[...], preferred_element_type=jnp.float32)
        total = term if total is None else total + term
    return total


def whole(array):
    return pl.BlockSpec(array.shape, lambda i: (0, 0))


def tiles_of(array, width, place, tile):
    first = 0 if array.shape[1] == width else place // tile
    return pl.BlockSpec((array.shape[0], tile), lambda i: (0, first + i))


def sum_for_outer(left, place, *rows):
    def kernel(left_ref, *refs):
        refs[-1][...] = block_sum(left_ref, refs[:-1]).astype(jnp.bfloat16)

    tok, width = rows[-1].shape
    tile = width // 2 if place == 0 and width % 256 == 0 else tile_of(place, width)
    return pl.pallas_call(
        kernel,
        grid=(width // tile,),
        out_shape=jax.ShapeDtypeStruct((left.shape[0], width), jnp.bfloat16),
        in_specs=[whole(left)] + [tiles_of(array, width, place, tile) for array in rows],
        out_specs=pl.BlockSpec((left.shape[0], tile), lambda i: (0, i)),
        compiler_params=pltpu.CompilerParams(vmem_limit_bytes=32 << 20),
        cost_estimate=COST,
        name="sum_for_outer",
    )(left, *rows)


def own_rows(left, place, rows, got, total, mark, start, columns, share):
    width = got.shape[1]
    tile = min(tile_of(start, width), tile_of(place, width))
    before = [] if total is None else [total, mark]

    def kernel(left_ref, *refs):
        here = block_sum(left_ref, refs[:4])
        refs[-2][...] = (here + refs[4][...].astype(jnp.float32)) * (1.0 / share)
        refs[-1][...] = jnp.zeros(refs[-1].shape, jnp.float32)

    return pl.pallas_call(
        kernel,
        grid=(width // tile,),
        out_shape=[
            jax.ShapeDtypeStruct((left.shape[0], columns), jnp.float32),
            jax.ShapeDtypeStruct((8, 128), jnp.float32),
        ],
        in_specs=[whole(left)]
        + [tiles_of(array, width, place, tile) for array in (*rows, got)]
        + [pl.BlockSpec(memory_space=pl.ANY)] * len(before),
        out_specs=[
            pl.BlockSpec((left.shape[0], tile), lambda i: (0, start // tile + i)),
            pl.BlockSpec((8, 128), lambda i: (0, 0)),
        ],
        input_output_aliases={6: 0} if before else {},
        compiler_params=pltpu.CompilerParams(vmem_limit_bytes=32 << 20),
        cost_estimate=COST,
        name="own_rows",
    )(left, *rows, got, *before)


def by_gathering(acts, out_grads, lengths):
    blocks = lax.axis_size("dp")
    norms, token_factor = norms_and_factors(acts, out_grads, lengths)
    rows = lax.all_gather(weigh(token_factor, out_grads), "dp", axis=0, tiled=True)
    mine = lax.all_to_all(acts, "dp", split_axis=1, concat_axis=0, tiled=True)
    return (outer_rows(mine, rows) / (lengths.shape[1] * blocks), norms[None, :])


def on_line_of_four(acts, out_grads, lengths):
    tok, width = acts.shape[0], acts.shape[1] // 4
    z = lax.axis_index("dp")
    side = z // 2
    outer = 3 * side
    share = tok // lax.axis_size("mp")
    part = lax.dynamic_slice_in_dim(acts, lax.axis_index("mp") * share, share, axis=0)
    other_half = lax.dynamic_slice_in_dim(part, (1 - side) * 2 * width, 2 * width, axis=1)
    inner_rows = lax.dynamic_slice_in_dim(part, (1 + side) * width, width, axis=1)

    starts = [sum(WIDTHS[:j]) for j in range(len(WIDTHS))]
    pieces = [(j, 0, width) for j, width in enumerate(WIDTHS[:-1])]
    pieces += [(len(WIDTHS) - 1, sum(LAST[:i]), width) for i, width in enumerate(LAST)]
    own, across = {}, {}

    crossed = []
    due = [[] for _ in range(2 * len(pieces) + 24)]

    def cross(array, before=2):
        at = len(crossed)
        crossed.append(lax.ppermute(after(array, crossed[at - before : at - before + 1], due[at]), "dp", ACROSS))
        return crossed[-1]

    def bring(j):
        own[j] = (weighted if j else weigh(f_own, out_grads))[:, starts[j] : starts[j] + WIDTHS[j]]
        across[j] = cross(own[j])

    def from_outside(j, place, width):
        rows = own[j]
        if width < WIDTHS[j]:
            rows = weighted[:, starts[j] + place : starts[j] + place + width]
        return lax.ppermute(after(rows, crossed[-3:-2]), "dp", TO_INNER)

    def columns(array, start):
        return lax.dynamic_slice_in_dim(array, start * width, width, axis=1)

    a_relayed = lax.ppermute(other_half, "dp", TO_INNER)
    a_across = cross(other_half)
    norms, f_own = norms_and_factors(acts, out_grads, lengths, [a_relayed])
    a_near = lax.ppermute(after(inner_rows, [a_relayed]), "dp", TO_INNER)
    a_far = cross(a_relayed)
    met = lax.all_gather(
        jnp.concatenate([after(a_across, [f_own]), a_far, a_near], axis=1), "mp", axis=0, tiled=True
    )
    mine, theirs = 1 - side, side
    left_mine = jnp.concatenate(
        [columns(acts, z), columns(met, mine), columns(met, 2 + mine), met[:, 4 * width :]], axis=0
    ).T
    left_theirs = jnp.concatenate(
        [columns(acts, outer), columns(met, theirs), columns(met, 2 + theirs)], axis=0
    ).T

    bring(0)
    near = [from_outside(*pieces[0])]
    weighted = weigh(f_own, after(out_grads, [f_own]))
    bring(1)
    near += [from_outside(*piece) for piece in pieces[1:] if piece[0] == 1]
    total = mark = None
    gots = []
    for i, (j, place, width) in enumerate(pieces):
        at = len(crossed)
        last = j == len(WIDTHS) - 1
        far = cross(near[i], 2 if not last or i == len(pieces) - 1 and len(LAST) > 2 else LAST_WAITS[place > 0])
        if j + 2 < len(WIDTHS):
            bring(j + 2)
            near += [from_outside(*piece) for piece in pieces if piece[0] == j + 2]
        sent = sum_for_outer(left_theirs, place, own[j], across[j], far)
        got = lax.ppermute(after(sent, gots[-1:]), "dp", TO_OUTER)
        gots.append(got)
        total, mark = own_rows(
            left_mine, place, (own[j], across[j], far, near[i]), got, total, mark, starts[j] + place,
            out_grads.shape[1], 4 * lengths.shape[1],
        )
        late = max(0, 2 - j) * LATE
        for later, array in ((SENT, sent), (GOT, got), (DONE, mark)):
            if at + later + late <= 2 * len(WIDTHS) + END:
                due[at + later + late] += [array]
    return (total, norms[None, :])


def solution(mesh):
    in_specs = (P(("groups", "dp"), None), P(("groups", "dp"), "mp"), P(("groups", "dp"), None))
    out_specs = (P(("groups", "dp"), "mp"), P(("groups", "dp"), None))
    on_device = on_line_of_four if mesh.shape["dp"] == 4 else by_gathering
    return jax.shard_map(
        on_device, mesh=mesh, in_specs=in_specs, out_specs=out_specs, check_vma=False
    )
```

```python
import math

import jax
import jax.numpy as jnp
from jax import lax
from jax.experimental import pallas as pl
from jax.experimental.pallas import tpu as pltpu
from jax.sharding import PartitionSpec as P

D = 2304
FFW = 18432
MOST = 256

TO_INNER = [(0, 1), (3, 2)]
ACROSS = [(1, 2), (2, 1)]
TO_OUTER = [(1, 0), (2, 3)]
WIDTHS = (1024,768,768,768,768,512)
LAST = (512,)
LAST_WAITS = (1,1)
END = 99
LATE = 1
SENT, GOT, DONE = 4,6,4

COST = pl.CostEstimate(flops=0, bytes_accessed=0, transcendentals=0)


def bound():
    return math.sqrt(D * FFW * MOST) / 2.0


def outer_rows(left, right):
    return lax.dot_general(
        left, right, (((0,), (0,)), ((), ())), preferred_element_type=jnp.float32
    )


def gram_steps(acts, out_grads):
    for steps in (2, 1):
        if acts.shape[1] % (steps * 128) == 0 and out_grads.shape[1] % (steps * 128) == 0:
            return steps
    return 1


def squared_norms(acts, out_grads, lengths):
    tok, segments = acts.shape[0], lengths.shape[1]
    steps = gram_steps(acts, out_grads)
    half = tok // 2
    quarters = ((0, 0), (half, 0), (half, half))

    def kernel(lengths_ref, acts_ref, grads_ref, out_ref, member_ref, act_gram, grad_gram):
        step = pl.program_id(0)

        def add(first):
            for rows_ref, gram in ((acts_ref, act_gram), (grads_ref, grad_gram)):
                rows = rows_ref[...]
                for top, left in quarters:
                    place = (slice(top, top + half), slice(left, left + half))
                    term = lax.dot_general(
                        rows[top : top + half],
                        rows[left : left + half],
                        (((1,), (1,)), ((), ())),
                        preferred_element_type=jnp.float32,
                    )
                    gram[place] = term if first else gram[place] + term

        pl.when(step == 0)(lambda: add(True))
        pl.when(step > 0)(lambda: add(False))

        @pl.when(step == steps - 1)
        def _():
            squared = jnp.zeros((1, 128), jnp.float32)
            lane = lax.broadcasted_iota(jnp.int32, (1, 128), 1)
            for top, left in quarters:
                of_row = jnp.zeros((half, 1), jnp.int32)
                of_column = jnp.zeros((1, half), jnp.int32)
                end = 0
                for j in range(segments):
                    end += lengths_ref[0, j]
                    of_row += (top + lax.broadcasted_iota(jnp.int32, (half, 1), 0) >= end).astype(jnp.int32)
                    of_column += (left + lax.broadcasted_iota(jnp.int32, (1, half), 1) >= end).astype(jnp.int32)
                place = (slice(top, top + half), slice(left, left + half))
                product = jnp.where(of_row == of_column, act_gram[place] * grad_gram[place], 0.0)
                per_token = jnp.sum(product, axis=1, keepdims=True) * (1.0 if top == left else 2.0)
                squared += jnp.sum(jnp.where(of_row == lane, per_token, 0.0), axis=0, keepdims=True)
                if top == left:
                    member_ref[top : top + half] = (of_row == lane).astype(jnp.float32)
            out_ref[...] = squared

    return pl.pallas_call(
        kernel,
        grid=(steps,),
        out_shape=[jax.ShapeDtypeStruct((1, 128), jnp.float32), jax.ShapeDtypeStruct((tok, 128), jnp.float32)],
        in_specs=[
            pl.BlockSpec(memory_space=pltpu.SMEM),
            pl.BlockSpec((tok, acts.shape[1] // steps), lambda i: (0, i)),
            pl.BlockSpec((tok, out_grads.shape[1] // steps), lambda i: (0, i)),
        ],
        out_specs=[pl.BlockSpec((1, 128), lambda i: (0, 0)), pl.BlockSpec((tok, 128), lambda i: (0, 0))],
        scratch_shapes=[pltpu.VMEM((tok, tok), jnp.float32)] * 2,
        compiler_params=pltpu.CompilerParams(vmem_limit_bytes=56 << 20),
        cost_estimate=pl.CostEstimate(
            flops=2 * tok * (acts.size + out_grads.size),
            bytes_accessed=2 * (acts.size + out_grads.size),
            transcendentals=0,
        ),
        name="squared_norms",
    )(lengths, acts, out_grads)


def norms_and_factors(acts, out_grads, lengths, *others):
    squared, member = squared_norms(acts, out_grads, lengths)
    norms = jnp.sqrt(lax.psum(after(squared, others), "mp"))
    factor = jnp.minimum(1.0, bound() / (norms + 1e-06))
    return norms[0, : lengths.shape[1]], jnp.sum(member * factor, axis=1)


def after(array, *others):
    return lax.optimization_barrier((array, *(o for some in others for o in some)))[0]


def weigh(token_factor, rows):
    return (token_factor[:, None] * rows.astype(jnp.float32)).astype(jnp.bfloat16)


def tile_of(start, width):
    return 256 if start % 256 == 0 and width % 256 == 0 else 128


def block_sum(left_ref, rows_refs):
    tok = rows_refs[0].shape[0]
    total = None
    for i, rows_ref in enumerate(rows_refs):
        term = jnp.dot(left_ref[:, i * tok : (i + 1) * tok], rows_ref[...], preferred_element_type=jnp.float32)
        total = term if total is None else total + term
    return total


def whole(array):
    return pl.BlockSpec(array.shape, lambda i: (0, 0))


def tiles_of(array, width, place, tile):
    first = 0 if array.shape[1] == width else place // tile
    return pl.BlockSpec((array.shape[0], tile), lambda i: (0, first + i))


def sum_for_outer(left, place, *rows):
    def kernel(left_ref, *refs):
        refs[-1][...] = block_sum(left_ref, refs[:-1]).astype(jnp.bfloat16)

    tok, width = rows[-1].shape
    tile = width // 2 if place == 0 and width % 256 == 0 else tile_of(place, width)
    return pl.pallas_call(
        kernel,
        grid=(width // tile,),
        out_shape=jax.ShapeDtypeStruct((left.shape[0], width), jnp.bfloat16),
        in_specs=[whole(left)] + [tiles_of(array, width, place, tile) for array in rows],
        out_specs=pl.BlockSpec((left.shape[0], tile), lambda i: (0, i)),
        compiler_params=pltpu.CompilerParams(vmem_limit_bytes=32 << 20),
        cost_estimate=COST,
        name="sum_for_outer",
    )(left, *rows)


def own_rows(left, place, rows, got, total, mark, start, columns, share):
    width = got.shape[1]
    tile = min(tile_of(start, width), tile_of(place, width))
    before = [] if total is None else [total, mark]

    def kernel(left_ref, *refs):
        here = block_sum(left_ref, refs[:4])
        refs[-2][...] = (here + refs[4][...].astype(jnp.float32)) * (1.0 / share)
        refs[-1][...] = jnp.zeros(refs[-1].shape, jnp.float32)

    return pl.pallas_call(
        kernel,
        grid=(width // tile,),
        out_shape=[
            jax.ShapeDtypeStruct((left.shape[0], columns), jnp.float32),
            jax.ShapeDtypeStruct((8, 128), jnp.float32),
        ],
        in_specs=[whole(left)]
        + [tiles_of(array, width, place, tile) for array in (*rows, got)]
        + [pl.BlockSpec(memory_space=pl.ANY)] * len(before),
        out_specs=[
            pl.BlockSpec((left.shape[0], tile), lambda i: (0, start // tile + i)),
            pl.BlockSpec((8, 128), lambda i: (0, 0)),
        ],
        input_output_aliases={6: 0} if before else {},
        compiler_params=pltpu.CompilerParams(vmem_limit_bytes=32 << 20),
        cost_estimate=COST,
        name="own_rows",
    )(left, *rows, got, *before)


def by_gathering(acts, out_grads, lengths):
    blocks = lax.axis_size("dp")
    norms, token_factor = norms_and_factors(acts, out_grads, lengths)
    rows = lax.all_gather(weigh(token_factor, out_grads), "dp", axis=0, tiled=True)
    mine = lax.all_to_all(acts, "dp", split_axis=1, concat_axis=0, tiled=True)
    return (outer_rows(mine, rows) / (lengths.shape[1] * blocks), norms[None, :])


def on_line_of_four(acts, out_grads, lengths):
    tok, width = acts.shape[0], acts.shape[1] // 4
    z = lax.axis_index("dp")
    side = z // 2
    outer = 3 * side
    share = tok // lax.axis_size("mp")
    part = lax.dynamic_slice_in_dim(acts, lax.axis_index("mp") * share, share, axis=0)
    other_half = lax.dynamic_slice_in_dim(part, (1 - side) * 2 * width, 2 * width, axis=1)
    inner_rows = lax.dynamic_slice_in_dim(part, (1 + side) * width, width, axis=1)

    starts = [sum(WIDTHS[:j]) for j in range(len(WIDTHS))]
    pieces = [(j, 0, width) for j, width in enumerate(WIDTHS[:-1])]
    pieces += [(len(WIDTHS) - 1, sum(LAST[:i]), width) for i, width in enumerate(LAST)]
    own, across = {}, {}

    crossed = []
    due = [[] for _ in range(2 * len(pieces) + 24)]

    def cross(array, before=2):
        at = len(crossed)
        crossed.append(lax.ppermute(after(array, crossed[at - before : at - before + 1], due[at]), "dp", ACROSS))
        return crossed[-1]

    def bring(j):
        own[j] = (weighted if j else weigh(f_own, out_grads))[:, starts[j] : starts[j] + WIDTHS[j]]
        across[j] = cross(own[j])

    def from_outside(j, place, width):
        rows = own[j]
        if width < WIDTHS[j]:
            rows = weighted[:, starts[j] + place : starts[j] + place + width]
        return lax.ppermute(after(rows, crossed[-3:-2]), "dp", TO_INNER)

    def columns(array, start):
        return lax.dynamic_slice_in_dim(array, start * width, width, axis=1)

    a_relayed = lax.ppermute(other_half, "dp", TO_INNER)
    a_across = cross(other_half)
    norms, f_own = norms_and_factors(acts, out_grads, lengths, [a_relayed])
    a_near = lax.ppermute(after(inner_rows, [a_relayed]), "dp", TO_INNER)
    a_far = cross(a_relayed)
    met = lax.all_gather(
        jnp.concatenate([after(a_across, [f_own]), a_far, a_near], axis=1), "mp", axis=0, tiled=True
    )
    mine, theirs = 1 - side, side
    left_mine = jnp.concatenate(
        [columns(acts, z), columns(met, mine), columns(met, 2 + mine), met[:, 4 * width :]], axis=0
    ).T
    left_theirs = jnp.concatenate(
        [columns(acts, outer), columns(met, theirs), columns(met, 2 + theirs)], axis=0
    ).T

    bring(0)
    near = [from_outside(*pieces[0])]
    weighted = weigh(f_own, after(out_grads, [f_own]))
    bring(1)
    near += [from_outside(*piece) for piece in pieces[1:] if piece[0] == 1]
    total = mark = None
    gots = []
    for i, (j, place, width) in enumerate(pieces):
        at = len(crossed)
        last = j == len(WIDTHS) - 1
        far = cross(near[i], 2 if not last or i == len(pieces) - 1 and len(LAST) > 2 else LAST_WAITS[place > 0])
        if j + 2 < len(WIDTHS):
            bring(j + 2)
            near += [from_outside(*piece) for piece in pieces if piece[0] == j + 2]
        sent = sum_for_outer(left_theirs, place, own[j], across[j], far)
        got = lax.ppermute(after(sent, gots[-1:]), "dp", TO_OUTER)
        gots.append(got)
        total, mark = own_rows(
            left_mine, place, (own[j], across[j], far, near[i]), got, total, mark, starts[j] + place,
            out_grads.shape[1], 4 * lengths.shape[1],
        )
        late = max(0, 2 - j) * LATE
        for later, array in ((SENT, sent), (GOT, got), (DONE, mark)):
            if at + later + late <= 2 * len(WIDTHS) + END:
                due[at + later + late] += [array]
    return (total, norms[None, :])


def solution(mesh):
    in_specs = (P(("groups", "dp"), None), P(("groups", "dp"), "mp"), P(("groups", "dp"), None))
    out_specs = (P(("groups", "dp"), "mp"), P(("groups", "dp"), None))
    on_device = on_line_of_four if mesh.shape["dp"] == 4 else by_gathering
    return jax.shard_map(
        on_device, mesh=mesh, in_specs=in_specs, out_specs=out_specs, check_vma=False
    )
```
